32 devices in a mesh: layer: 4 (over x, core), feat: 8 (over z, y).
Axes of the slice: x: 2, y: 2, z: 4, core: 2. Of those that a mesh axis runs over, the one named last changes fastest.
Arguments:
- sources: bfloat16 [4, 512, 4096], P('layer', 'feat'), may hold values from -6 to 6
- targets: bfloat16 [4, 512, 4096], P('layer', 'feat'), may hold values from -6 to 6
- enc_weight: bfloat16 [4, 8192, 4096], P('layer', 'feat'), may hold values from -0.09375 to 0.09375
- dec_weight: bfloat16 [4, 4, 8192, 4096], P('layer', None, 'feat'), may hold values from -0.0625 to 0.0625
- active: int32 [4, 8192, 512], P('layer', 'feat'), may hold values 0 or 1
Outputs:
- errors: float32 [4, 512, 4096], P('layer', 'feat')
- grad_dec: bfloat16 [4, 4, 8192, 4096], P('layer', None, 'feat')
- grad_enc: bfloat16 [4, 8192, 4096], P('layer', 'feat')
The draws below stay inside these ranges and needn't reach their ends.
All inputs are finite; a program needn't handle non-finite values. No bound on the sum of `active` on one device may be relied on, other than what follows from the above.
Results may differ from the reference program's by a relative error of at most 0.0061.
Values may be sent and summed in bfloat16 or wider, within the bound.
A program may use at most 192 MiB of HBM per device.

```python
import math
import jax
import jax.numpy as jnp

D = 4096
F = 8192
TOKENS = 512
LAYERS = 4


def set_ends(entries, own_key, low, largest):
    place = [jax.random.randint(jax.random.fold_in(own_key, axis), (), 0, length) for axis, length in enumerate(entries.shape)]
    longest = entries.shape.index(max(entries.shape))
    neighbour = place[:longest] + [(place[longest] + 1) % entries.shape[longest]] + place[longest + 1:]
    return entries.at[tuple(place)].set(low).at[tuple(neighbour)].set(largest)


def level_of(stream_key, dims, cuts, smallest, high):
    gain, own = 1.0, jax.random.fold_in(stream_key, 6)
    for dim, blocks in cuts:
        steps = jnp.exp(jax.random.uniform(jax.random.fold_in(own, dim), (blocks,), jnp.float32, smallest / len(cuts), high / len(cuts)))
        gain = gain * jnp.repeat(steps, dims[dim] // blocks).reshape([-1 if axis == dim else 1 for axis in range(len(dims))])
    return gain


def noise(own_key, dims, width, most, pieces=(), dtype=jnp.bfloat16):
    values = jax.random.normal(own_key, dims, jnp.float32) * width
    if len(pieces) > 0:
        values = level_of(own_key, dims, pieces, -0.22, 0.18) * values
    return jnp.clip(values, min=-most, max=most).astype(dtype)


def setup_inputs(seed: int = 0) -> dict:
    keys = jax.random.split(jax.random.key(seed), 6)
    sources = noise(keys[0], (LAYERS, TOKENS, D), 1.0, 6.0, ((0, 4), (1, 8)))
    targets = noise(keys[1], (LAYERS, TOKENS, D), 1.0, 6.0, ((0, 4), (1, 8)))
    enc_weight = noise(keys[2], (LAYERS, F, D), D ** -0.5, 0.09375, ((0, 4), (1, 8)))
    dec_weight = noise(keys[3], (LAYERS, LAYERS, F, D), F ** -0.5, 0.0625, ((0, 4), (2, 8)))
    active = set_ends((jax.random.randint(keys[4], (LAYERS, F, TOKENS), 0, 5) < 2).astype(jnp.int32), jax.random.fold_in(keys[4], 1), 0, 1)
    return dict(sources=sources, targets=targets, enc_weight=enc_weight, dec_weight=dec_weight, active=active)


def reference(sources, targets, enc_weight, dec_weight, active):
    pre_acts = jnp.einsum('lfd,ltd->lft', enc_weight.astype(jnp.float32), sources.astype(jnp.float32))
    features = (active.astype(jnp.float32) * pre_acts).astype(jnp.bfloat16)
    scale = 1.0 / math.sqrt(TOKENS)
    error_list = []
    for target in range(LAYERS):
        recon = jnp.zeros((TOKENS, D), jnp.float32)
        for source in range(target + 1):
            recon = recon + jnp.dot(features[source].T, dec_weight[target, source], preferred_element_type=jnp.float32)
        error_list.append(recon - targets[target].astype(jnp.float32))
    errors = jnp.stack(error_list)
    scaled_error = (errors * scale).astype(jnp.bfloat16)
    dec_rows = []
    for target in range(LAYERS):
        blocks = []
        for source in range(LAYERS):
            if source <= target:
                blocks.append(jnp.dot(features[source], scaled_error[target], preferred_element_type=jnp.float32).astype(jnp.bfloat16))
            else:
                blocks.append(jnp.zeros((F, D), jnp.bfloat16))
        dec_rows.append(jnp.stack(blocks))
    grad_dec = jnp.stack(dec_rows)
    enc_list = []
    for source in range(LAYERS):
        feature_grad = jnp.zeros((F, TOKENS), jnp.float32)
        for target in range(source, LAYERS):
            feature_grad = feature_grad + jnp.dot(dec_weight[target, source], scaled_error[target].T, preferred_element_type=jnp.float32)
        pre_grad = (active[source].astype(jnp.float32) * feature_grad).astype(jnp.bfloat16)
        enc_list.append(jnp.dot(pre_grad, sources[source], preferred_element_type=jnp.float32).astype(jnp.bfloat16))
    grad_enc = jnp.stack(enc_list)
    return (errors, grad_dec, grad_enc)
```

```python
import functools
import math

import jax
import jax.numpy as jnp
from jax import lax
from jax.experimental import pallas as pl
from jax.experimental.pallas import tpu as pltpu
from jax.sharding import PartitionSpec as P

MESH = pl.DeviceIdType.MESH
VMEM_LIMIT = 40 * 1024 * 1024


def place(axis, count):
    me = lax.axis_index(axis)
    return me, me // 2, lax.rem(me, 2), count // 2


def greet(axis, count):
    me, z, y, length = place(axis, count)
    barrier = pltpu.get_barrier_semaphore()

    def signal(device):
        pl.semaphore_signal(barrier, inc=1, device_id={axis: device}, device_id_type=MESH)

    signal(me + 1 - 2 * y)
    pl.when(z > 0)(lambda: signal(me - 2))
    pl.when(z < length - 1)(lambda: signal(me + 2))
    pl.semaphore_wait(barrier, 1 + (z > 0).astype(jnp.int32) + (z < length - 1).astype(jnp.int32))


def gather(axis, count, causal, own, out, line_sem, side_sem, recv_sem):
    me, z, y, length = place(axis, count)
    other = 1 - y

    def copy(block, source, device, sem):
        return pltpu.make_async_remote_copy(
            src_ref=source, dst_ref=out.at[block], send_sem=sem, recv_sem=recv_sem.at[block],
            device_id={axis: device}, device_id_type=MESH)

    def across(line, source):
        return copy(line * 2 + y, source, z * 2 + other, side_sem.at[line])

    def right(line, source):
        return copy(line * 2 + y, source, me + 2, line_sem.at[0, line])

    def left(line, source):
        return copy(line * 2 + y, source, me - 2, line_sem.at[1, line])

    def arrived(block):
        copy(block, own, me, side_sem.at[0]).wait_recv()

    def own_across():
        return (y == 0) if causal else (y >= 0)

    pl.when(z < length - 1)(lambda: right(z, own).start())
    if not causal:
        pl.when(z > 0)(lambda: left(z, own).start())
    pl.when(own_across())(lambda: across(z, own).start())
    for step in range(1, length):
        @pl.when(z - step >= 0)
        def _():
            line = z - step
            block = line * 2 + y
            arrived(block)
            pl.when(z < length - 1)(lambda: right(line, out.at[block]).start())
            across(line, out.at[block]).start()

        if not causal:
            @pl.when(z + step < length)
            def _():
                line = z + step
                block = line * 2 + y
                arrived(block)
                pl.when(z > 0)(lambda: left(line, out.at[block]).start())
                across(line, out.at[block]).start()

    for line in range(length):
        @pl.when((line < z) | ((line == z) & (y == 1)) if causal else (z >= 0))
        def _():
            arrived(line * 2 + other)

        @pl.when((line < z) | ((line == z) & (y == 0)) if causal else (z >= 0))
        def _():
            across(line, own).wait_send()

        pl.when((line <= z) & (z < length - 1))(lambda: right(line, own).wait_send())
        if not causal:
            pl.when((line >= z) & (z > 0))(lambda: left(line, own).wait_send())


def gather_sems(count):
    return [
        pltpu.SemaphoreType.DMA((2, count // 2)),
        pltpu.SemaphoreType.DMA((count // 2,)),
        pltpu.SemaphoreType.DMA((count,)),
    ]


def gather_kernel(axis, count, causal, own, out, local_sem, line_sem, side_sem, recv_sem):
    me = lax.axis_index(axis)
    local = pltpu.make_async_copy(own, out.at[me], local_sem)
    local.start()
    greet(axis, count)
    gather(axis, count, causal, own, out, line_sem, side_sem, recv_sem)
    local.wait()


def gather_call(block, axis, causal, collective_id):
    count = lax.axis_size(axis)
    return pl.pallas_call(
        functools.partial(gather_kernel, axis, count, causal),
        out_shape=jax.ShapeDtypeStruct((count,) + block.shape, block.dtype),
        in_specs=[pl.BlockSpec(memory_space=pl.ANY)],
        out_specs=pl.BlockSpec(memory_space=pl.ANY),
        scratch_shapes=[pltpu.SemaphoreType.DMA(())] + gather_sems(count),
        compiler_params=pltpu.CompilerParams(collective_id=collective_id, has_side_effects=True),
    )(block)


def reduce_kernel(
    axis, count, scale, parts, targets, errors, full,
    from_side, from_left, from_right, to_right, to_left, scaled,
    local_sem, line_sem, side_sem, recv_sem,
    side_send, side_recv, right_send, right_recv, left_send, left_recv,
):
    me, z, y, length = place(axis, count)
    rows = targets.shape[0]
    step_rows = min(16, rows)
    greet(axis, count)

    def copy(source, target, send_sem, recv, device):
        return pltpu.make_async_remote_copy(
            src_ref=source, dst_ref=target, send_sem=send_sem, recv_sem=recv,
            device_id={axis: device}, device_id_type=MESH)

    def side(line):
        return copy(parts.at[line * 2 + 1 - y], from_side.at[line], side_send.at[line],
                    side_recv.at[line], me + 1 - 2 * y)

    def right(line):
        return copy(to_right.at[line], from_left.at[line], right_send.at[line],
                    right_recv.at[line], me + 2)

    def left(line):
        return copy(to_left.at[line], from_right.at[line], left_send.at[line],
                    left_recv.at[line], me - 2)

    for step in range(length - 1):
        pl.when(length - 1 - step > z)(lambda: side(length - 1 - step).start())
        pl.when(step < z)(lambda: side(step).start())
    side(z).start()

    def add(line, others, store):
        @pl.loop(0, rows // step_rows)
        def _(index):
            at = pl.ds(pl.multiple_of(index * step_rows, step_rows), step_rows)
            total = parts[line * 2 + y, at, :].astype(jnp.float32)
            for ref in others:
                total += ref[line, at, :].astype(jnp.float32)
            store(at, total)

    def pass_on(line, incoming, has_incoming, outgoing, message, recv):
        def store(at, total):
            outgoing[line, at, :] = total.astype(outgoing.dtype)

        side(line).wait_recv()

        @pl.when(has_incoming)
        def _():
            recv(line).wait_recv()
            add(line, (from_side, incoming), store)

        @pl.when(jnp.logical_not(has_incoming))
        def _():
            add(line, (from_side,), store)

        message(line).start()

    for step in range(length - 1):
        @pl.when(length - 1 - step > z)
        def _():
            pass_on(length - 1 - step, from_left, z > 0, to_right, right, right)

        @pl.when(step < z)
        def _():
            pass_on(step, from_right, z < length - 1, to_left, left, left)

    side(z).wait_recv()

    def finish(others):
        def store(at, total):
            error = total - targets[at, :].astype(jnp.float32)
            errors[at, :] = error
            scaled[at, :] = (error * scale).astype(scaled.dtype)

        add(z, others, store)

    @pl.when(z > 0)
    def _():
        right(z).wait_recv()

    @pl.when(z < length - 1)
    def _():
        left(z).wait_recv()

    pl.when((z > 0) & (z < length - 1))(lambda: finish((from_side, from_left, from_right)))
    pl.when((z > 0) & (z == length - 1))(lambda: finish((from_side, from_left)))
    pl.when((z == 0) & (z < length - 1))(lambda: finish((from_side, from_right)))
    pl.when((z == 0) & (z == length - 1))(lambda: finish((from_side,)))

    local = pltpu.make_async_copy(scaled, full.at[me], local_sem)
    local.start()
    gather(axis, count, False, scaled, full, line_sem, side_sem, recv_sem)
    local.wait()
    for line in range(length):
        side(line).wait_send()
        pl.when(line > z)(lambda: right(line).wait_send())
        pl.when(line < z)(lambda: left(line).wait_send())


def reduce_call(parts, targets, axis, scale, collective_id):
    count, rows, width = parts.shape
    length = count // 2
    lane = pltpu.VMEM((length, rows, width), parts.dtype)
    sems = pltpu.SemaphoreType.DMA((length,))
    vmem = pl.BlockSpec(memory_space=pltpu.VMEM)
    return pl.pallas_call(
        functools.partial(reduce_kernel, axis, count, scale),
        out_shape=(
            jax.ShapeDtypeStruct((rows, width), jnp.float32),
            jax.ShapeDtypeStruct((count, rows, width), parts.dtype),
        ),
        in_specs=[vmem, vmem],
        out_specs=(vmem, pl.BlockSpec(memory_space=pl.ANY)),
        scratch_shapes=[lane] * 5 + [pltpu.VMEM((rows, width), parts.dtype)]
        + [pltpu.SemaphoreType.DMA(())] + gather_sems(count) + [sems] * 6,
        compiler_params=pltpu.CompilerParams(
            collective_id=collective_id, has_side_effects=True, vmem_limit_bytes=VMEM_LIMIT),
    )(parts, targets)


def on_device(sources, targets, enc_weight, dec_weight, active):
    layer_count = dec_weight.shape[1]
    target_pos = lax.axis_index("layer")
    rows, width = sources.shape[1:]
    feat = lax.axis_size("feat")
    tokens = rows * feat
    source_full = gather_call(sources[0], "feat", False, 0).reshape(tokens, width)
    pre_acts = jnp.einsum(
        "fd,td->ft", enc_weight[0], source_full, preferred_element_type=jnp.float32
    )
    mask = active[0].astype(jnp.float32)
    features = (mask * pre_acts).astype(jnp.bfloat16)
    all_features = gather_call(features, "layer", True, 1)
    causal = (jnp.arange(layer_count, dtype=jnp.int32) <= target_pos)[:, None, None]
    masked = jnp.where(causal, all_features, jnp.zeros((), jnp.bfloat16))
    recon = jnp.einsum(
        "lft,lfd->td", masked, dec_weight[0], preferred_element_type=jnp.float32
    ).astype(jnp.bfloat16)
    errors, scaled = reduce_call(
        recon.reshape(feat, rows, width), targets[0], "feat", 1.0 / math.sqrt(tokens), 2
    )
    scaled_full = scaled.reshape(tokens, width)
    partial_grad = jnp.einsum(
        "lfd,td->lft", dec_weight[0], scaled_full, preferred_element_type=jnp.float32
    )
    partial_grad = jnp.where(causal, partial_grad, 0.0).astype(jnp.bfloat16)
    feature_grad = lax.psum_scatter(partial_grad, "layer", scatter_dimension=0, tiled=True)
    grad_dec = jnp.einsum(
        "lft,td->lfd", masked, scaled_full, preferred_element_type=jnp.float32
    ).astype(jnp.bfloat16)
    pre_grad = (mask * feature_grad[0].astype(jnp.float32)).astype(jnp.bfloat16)
    grad_enc = jnp.einsum(
        "ft,td->fd", pre_grad, source_full, preferred_element_type=jnp.float32
    ).astype(jnp.bfloat16)
    return (errors[None], grad_dec[None], grad_enc[None])


def solution(mesh):
    in_specs = (
        P("layer", "feat", None),
        P("layer", "feat", None),
        P("layer", "feat", None),
        P("layer", None, "feat", None),
        P("layer", "feat", None),
    )
    out_specs = (P("layer", "feat", None), P("layer", None, "feat", None), P("layer", "feat", None))
    return jax.shard_map(
        on_device, mesh=mesh, in_specs=in_specs, out_specs=out_specs, check_vma=False
    )
```

```python
import functools
import math

import jax
import jax.numpy as jnp
from jax import lax
from jax.experimental import pallas as pl
from jax.experimental.pallas import tpu as pltpu
from jax.sharding import PartitionSpec as P

MESH = pl.DeviceIdType.MESH
VMEM_LIMIT = 40 * 1024 * 1024


def place(axis, count):
    me = lax.axis_index(axis)
    return me, me // 2, lax.rem(me, 2), count // 2


def greet(axis, count):
    me, z, y, length = place(axis, count)
    barrier = pltpu.get_barrier_semaphore()

    def signal(device):
        pl.semaphore_signal(barrier, inc=1, device_id={axis: device}, device_id_type=MESH)

    signal(me + 1 - 2 * y)
    pl.when(z > 0)(lambda: signal(me - 2))
    pl.when(z < length - 1)(lambda: signal(me + 2))
    pl.semaphore_wait(barrier, 1 + (z > 0).astype(jnp.int32) + (z < length - 1).astype(jnp.int32))


def gather(axis, count, causal, own, out, line_sem, side_sem, recv_sem, work=None):
    me, z, y, length = place(axis, count)
    other = 1 - y

    def copy(block, source, device, sem):
        return pltpu.make_async_remote_copy(
            src_ref=source, dst_ref=out.at[block], send_sem=sem, recv_sem=recv_sem.at[block],
            device_id={axis: device}, device_id_type=MESH)

    def across(line, source):
        return copy(line * 2 + y, source, z * 2 + other, side_sem.at[line])

    def right(line, source):
        return copy(line * 2 + y, source, me + 2, line_sem.at[0, line])

    def left(line, source):
        return copy(line * 2 + y, source, me - 2, line_sem.at[1, line])

    def arrived(block):
        copy(block, own, me, side_sem.at[0]).wait_recv()

    def own_across():
        return (y == 0) if causal else (y >= 0)

    pl.when(z < length - 1)(lambda: right(z, own).start())
    if not causal:
        pl.when(z > 0)(lambda: left(z, own).start())
    pl.when(own_across())(lambda: across(z, own).start())
    for step in range(1, length):
        @pl.when(z - step >= 0)
        def _():
            line = z - step
            block = line * 2 + y
            arrived(block)
            pl.when(z < length - 1)(lambda: right(line, out.at[block]).start())
            across(line, out.at[block]).start()

        if not causal:
            @pl.when(z + step < length)
            def _():
                line = z + step
                block = line * 2 + y
                arrived(block)
                pl.when(z > 0)(lambda: left(line, out.at[block]).start())
                across(line, out.at[block]).start()

        if work is not None:
            if step == 1:
                work(z)
            else:
                pl.when(z - step + 1 >= 0)(lambda: work(z - step + 1))
                pl.when(z + step - 1 < length)(lambda: work(z + step - 1))

    if work is not None:
        last = length - 1
        if last == 0:
            work(z)
        else:
            pl.when(z - last >= 0)(lambda: work(z - last))
            pl.when(z + last < length)(lambda: work(z + last))

    for line in range(length):
        if work is None:
            @pl.when((line < z) | ((line == z) & (y == 1)) if causal else (z >= 0))
            def _():
                arrived(line * 2 + other)

        @pl.when((line < z) | ((line == z) & (y == 0)) if causal else (z >= 0))
        def _():
            across(line, own).wait_send()

        pl.when((line <= z) & (z < length - 1))(lambda: right(line, own).wait_send())
        if not causal:
            pl.when((line >= z) & (z > 0))(lambda: left(line, own).wait_send())


def gather_sems(count):
    return [
        pltpu.SemaphoreType.DMA((2, count // 2)),
        pltpu.SemaphoreType.DMA((count // 2,)),
        pltpu.SemaphoreType.DMA((count,)),
    ]


def encode_kernel(
    feat_count, layer_count, own, enc_hbm, mask, full_out, features_out,
    full, enc, features, local_sem, layer_sem, line_sem, side_sem, recv_sem,
    right_send, across_send, feature_recv,
):
    me, z, y, length = place("feat", feat_count)
    layer, chip, core, chips = place("layer", layer_count)
    rows, width = own.shape
    tile = min(256, enc.shape[0])
    group = 2 if rows % 16 == 0 else 1
    enc_copy = pltpu.make_async_copy(enc_hbm, enc, local_sem.at[0])
    enc_copy.start()
    own_copy = pltpu.make_async_copy(own, full.at[me], local_sem.at[1])
    own_copy.start()

    barrier = pltpu.get_barrier_semaphore()

    def signal(axis, device):
        pl.semaphore_signal(barrier, inc=1, device_id={axis: device}, device_id_type=MESH)

    signal("feat", me + 1 - 2 * y)
    signal("layer", layer + 1 - 2 * core)
    pl.when(z > 0)(lambda: signal("feat", me - 2))
    pl.when(z < length - 1)(lambda: signal("feat", me + 2))
    pl.when(chip > 0)(lambda: signal("layer", layer - 2))
    pl.when(chip < chips - 1)(lambda: signal("layer", layer + 2))
    pl.semaphore_wait(
        barrier,
        2 + (z > 0).astype(jnp.int32) + (z < length - 1).astype(jnp.int32)
        + (chip > 0).astype(jnp.int32) + (chip < chips - 1).astype(jnp.int32))

    def send(hop, line, sem, device):
        block = features.at[layer - 2 * hop, line]
        return pltpu.make_async_remote_copy(
            src_ref=block, dst_ref=block, send_sem=sem.at[hop, line],
            recv_sem=feature_recv.at[layer - 2 * hop, line],
            device_id={"layer": device}, device_id_type=MESH)

    def right(hop, line):
        return send(hop, line, right_send, layer + 2)

    def across(hop, line):
        return send(hop, line, across_send, layer + 1 - 2 * core)

    def landed(source, line):
        block = features.at[source, line]
        pltpu.make_async_remote_copy(
            src_ref=block, dst_ref=block, send_sem=right_send.at[0, line],
            recv_sem=feature_recv.at[source, line],
            device_id={"layer": layer}, device_id_type=MESH).wait_recv()

    def relay(line):
        for hop in range(1, chips):
            @pl.when(chip >= hop)
            def _():
                landed(layer - 2 * hop, line)
                pl.when(chip < chips - 1)(lambda: right(hop, line).start())
                across(hop, line).start()

    def work(line):
        pltpu.make_async_remote_copy(
            src_ref=own, dst_ref=full.at[line * 2 + 1 - y], send_sem=side_sem.at[0],
            recv_sem=recv_sem.at[line * 2 + 1 - y],
            device_id={"feat": me}, device_id_type=MESH).wait_recv()

        @pl.loop(0, enc.shape[0] // tile)
        def _(index):
            at = pl.ds(pl.multiple_of(index * tile, tile), tile)
            for part in range(2 // group):
                block = full[pl.ds(line * 2 + part, group)].reshape(group * rows, width)
                acts = lax.dot_general(
                    block, enc[at, :], (((1,), (1,)), ((), ())),
                    preferred_element_type=jnp.float32)
                tokens = pl.ds(part * rows, group * rows)
                kept = mask[line, tokens, at].astype(jnp.float32) * acts
                features[layer, line, tokens, at] = kept.astype(features.dtype)

        pl.when(chip < chips - 1)(lambda: right(0, line).start())
        pl.when(core == 0)(lambda: across(0, line).start())

    enc_copy.wait()
    own_copy.wait()
    gather("feat", feat_count, False, own, full, line_sem, side_sem, recv_sem, work)
    full_copy = pltpu.make_async_copy(full, full_out, local_sem.at[0])
    full_copy.start()
    relay(z)
    for step in range(1, length):
        pl.when(z - step >= 0)(lambda: relay(z - step))
        pl.when(z + step < length)(lambda: relay(z + step))
    for line in range(length):
        pl.when(core == 1)(lambda: landed(layer - 1, line))
        for hop in range(1, chips):
            pl.when(chip >= hop)(lambda: landed(layer - 2 * hop + 1 - 2 * core, line))
        for hop in range(chips):
            @pl.when(chip >= hop)
            def _():
                pl.when(chip < chips - 1)(lambda: right(hop, line).wait_send())
                if hop == 0:
                    pl.when(core == 0)(lambda: across(hop, line).wait_send())
                else:
                    across(hop, line).wait_send()

    def out_copy(source):
        return pltpu.make_async_copy(
            features.at[source], features_out.at[source], layer_sem.at[source])

    for source in range(layer_count):
        pl.when(source <= layer)(lambda: out_copy(source).start())
    for source in range(layer_count):
        pl.when(source <= layer)(lambda: out_copy(source).wait())
    full_copy.wait()


def encode_call(sources, enc_weight, mask, collective_id):
    count, layers = lax.axis_size("feat"), lax.axis_size("layer")
    rows, width = sources.shape
    size = enc_weight.shape[0]
    length, chips = count // 2, layers // 2
    hbm = pl.BlockSpec(memory_space=pl.ANY)
    full_shape = (count, rows, width)
    feature_shape = (layers, length, 2 * rows, size)
    return pl.pallas_call(
        functools.partial(encode_kernel, count, layers),
        out_shape=(
            jax.ShapeDtypeStruct(full_shape, sources.dtype),
            jax.ShapeDtypeStruct(feature_shape, sources.dtype),
        ),
        in_specs=[hbm, hbm, pl.BlockSpec(memory_space=pltpu.VMEM)],
        out_specs=(hbm, hbm),
        scratch_shapes=[
            pltpu.VMEM(full_shape, sources.dtype),
            pltpu.VMEM(enc_weight.shape, sources.dtype),
            pltpu.VMEM(feature_shape, sources.dtype),
            pltpu.SemaphoreType.DMA((2,)),
            pltpu.SemaphoreType.DMA((layers,)),
        ] + gather_sems(count) + [
            pltpu.SemaphoreType.DMA((chips, length)),
            pltpu.SemaphoreType.DMA((chips, length)),
            pltpu.SemaphoreType.DMA((layers, length)),
        ],
        compiler_params=pltpu.CompilerParams(
            collective_id=collective_id, has_side_effects=True, vmem_limit_bytes=VMEM_LIMIT),
    )(sources, enc_weight, mask.reshape(length, 2 * rows, size))


def reduce_kernel(
    axis, count, scale, parts, targets, errors, full,
    from_side, from_left, from_right, to_right, to_left, scaled,
    local_sem, line_sem, side_sem, recv_sem,
    side_send, side_recv, right_send, right_recv, left_send, left_recv,
):
    me, z, y, length = place(axis, count)
    rows = targets.shape[0]
    step_rows = min(16, rows)
    greet(axis, count)

    def copy(source, target, send_sem, recv, device):
        return pltpu.make_async_remote_copy(
            src_ref=source, dst_ref=target, send_sem=send_sem, recv_sem=recv,
            device_id={axis: device}, device_id_type=MESH)

    def side(line):
        return copy(parts.at[line * 2 + 1 - y], from_side.at[line], side_send.at[line],
                    side_recv.at[line], me + 1 - 2 * y)

    def right(line):
        return copy(to_right.at[line], from_left.at[line], right_send.at[line],
                    right_recv.at[line], me + 2)

    def left(line):
        return copy(to_left.at[line], from_right.at[line], left_send.at[line],
                    left_recv.at[line], me - 2)

    for step in range(length - 1):
        pl.when(length - 1 - step > z)(lambda: side(length - 1 - step).start())
        pl.when(step < z)(lambda: side(step).start())
    side(z).start()

    def add(line, others, store):
        @pl.loop(0, rows // step_rows)
        def _(index):
            at = pl.ds(pl.multiple_of(index * step_rows, step_rows), step_rows)
            total = parts[line * 2 + y, at, :].astype(jnp.float32)
            for ref in others:
                total += ref[line, at, :].astype(jnp.float32)
            store(at, total)

    def pass_on(line, incoming, has_incoming, outgoing, message, recv):
        def store(at, total):
            outgoing[line, at, :] = total.astype(outgoing.dtype)

        side(line).wait_recv()

        @pl.when(has_incoming)
        def _():
            recv(line).wait_recv()
            add(line, (from_side, incoming), store)

        @pl.when(jnp.logical_not(has_incoming))
        def _():
            add(line, (from_side,), store)

        message(line).start()

    for step in range(length - 1):
        @pl.when(length - 1 - step > z)
        def _():
            pass_on(length - 1 - step, from_left, z > 0, to_right, right, right)

        @pl.when(step < z)
        def _():
            pass_on(step, from_right, z < length - 1, to_left, left, left)

    side(z).wait_recv()

    def finish(others):
        def store(at, total):
            error = total - targets[at, :].astype(jnp.float32)
            errors[at, :] = error
            scaled[at, :] = (error * scale).astype(scaled.dtype)

        add(z, others, store)

    @pl.when(z > 0)
    def _():
        right(z).wait_recv()

    @pl.when(z < length - 1)
    def _():
        left(z).wait_recv()

    pl.when((z > 0) & (z < length - 1))(lambda: finish((from_side, from_left, from_right)))
    pl.when((z > 0) & (z == length - 1))(lambda: finish((from_side, from_left)))
    pl.when((z == 0) & (z < length - 1))(lambda: finish((from_side, from_right)))
    pl.when((z == 0) & (z == length - 1))(lambda: finish((from_side,)))

    local = pltpu.make_async_copy(scaled, full.at[me], local_sem)
    local.start()
    gather(axis, count, False, scaled, full, line_sem, side_sem, recv_sem)
    local.wait()
    for line in range(length):
        side(line).wait_send()
        pl.when(line > z)(lambda: right(line).wait_send())
        pl.when(line < z)(lambda: left(line).wait_send())


def reduce_call(parts, targets, axis, scale, collective_id):
    count, rows, width = parts.shape
    length = count // 2
    lane = pltpu.VMEM((length, rows, width), parts.dtype)
    sems = pltpu.SemaphoreType.DMA((length,))
    vmem = pl.BlockSpec(memory_space=pltpu.VMEM)
    return pl.pallas_call(
        functools.partial(reduce_kernel, axis, count, scale),
        out_shape=(
            jax.ShapeDtypeStruct((rows, width), jnp.float32),
            jax.ShapeDtypeStruct((count, rows, width), parts.dtype),
        ),
        in_specs=[vmem, vmem],
        out_specs=(vmem, pl.BlockSpec(memory_space=pl.ANY)),
        scratch_shapes=[lane] * 5 + [pltpu.VMEM((rows, width), parts.dtype)]
        + [pltpu.SemaphoreType.DMA(())] + gather_sems(count) + [sems] * 6,
        compiler_params=pltpu.CompilerParams(
            collective_id=collective_id, has_side_effects=True, vmem_limit_bytes=VMEM_LIMIT),
    )(parts, targets)


def scatter_layers(partial):
    layers = lax.axis_size("layer")
    layer, chip, core, chips = place("layer", layers)
    pairs = partial.reshape((chips, 2) + partial.shape[1:])
    swap = [(device, device ^ 1) for device in range(layers)]
    given = lax.ppermute(lax.dynamic_index_in_dim(pairs, 1 - core, 1, keepdims=False), "layer", swap)
    kept = lax.dynamic_index_in_dim(pairs, core, 1, keepdims=False)
    sums = (kept.astype(jnp.float32) + given.astype(jnp.float32)).astype(partial.dtype)
    total = lax.dynamic_index_in_dim(sums, chip, 0, keepdims=False).astype(jnp.float32)
    for shift in range(1, chips):
        target = lax.rem(chip + shift, chips)
        moves = [(device, (device + 2 * shift) % layers) for device in range(layers)]
        sent = lax.dynamic_index_in_dim(sums, target, 0, keepdims=False)
        total += lax.ppermute(sent, "layer", moves).astype(jnp.float32)
    return total


def on_device(sources, targets, enc_weight, dec_weight, active):
    layer_count = dec_weight.shape[1]
    target_pos = lax.axis_index("layer")
    rows, width = sources.shape[1:]
    feat = lax.axis_size("feat")
    tokens = rows * feat
    mask = active[0].astype(jnp.bfloat16).T
    source_full, all_features = encode_call(sources[0], enc_weight[0], mask, 0)
    source_full = source_full.reshape(tokens, width)
    all_features = all_features.reshape(layer_count, tokens, -1)
    causal = (jnp.arange(layer_count, dtype=jnp.int32) <= target_pos)[:, None, None]
    masked = jnp.where(causal, all_features, jnp.zeros((), jnp.bfloat16))
    recon = jnp.einsum(
        "ltf,lfd->td", masked, dec_weight[0], preferred_element_type=jnp.float32
    ).astype(jnp.bfloat16)
    errors, scaled = reduce_call(
        recon.reshape(feat, rows, width), targets[0], "feat", 1.0 / math.sqrt(tokens), 2
    )
    scaled_full = scaled.reshape(tokens, width)
    partial_grad = jnp.einsum(
        "lfd,td->ltf", dec_weight[0], scaled_full, preferred_element_type=jnp.float32
    )
    partial_grad = jnp.where(causal, partial_grad, 0.0).astype(jnp.bfloat16)
    feature_grad = scatter_layers(partial_grad)
    grad_dec = jnp.einsum(
        "ltf,td->lfd", masked, scaled_full, preferred_element_type=jnp.float32
    ).astype(jnp.bfloat16)
    pre_grad = (mask.astype(jnp.float32) * feature_grad).astype(jnp.bfloat16)
    grad_enc = jnp.einsum(
        "tf,td->fd", pre_grad, source_full, preferred_element_type=jnp.float32
    ).astype(jnp.bfloat16)
    return (errors[None], grad_dec[None], grad_enc[None])


def solution(mesh):
    in_specs = (
        P("layer", "feat", None),
        P("layer", "feat", None),
        P("layer", "feat", None),
        P("layer", None, "feat", None),
        P("layer", "feat", None),
    )
    out_specs = (P("layer", "feat", None), P("layer", None, "feat", None), P("layer", "feat", None))
    return jax.shard_map(
        on_device, mesh=mesh, in_specs=in_specs, out_specs=out_specs, check_vma=False
    )
```

```python
import functools
import math

import jax
import jax.numpy as jnp
from jax import lax
from jax.experimental import pallas as pl
from jax.experimental.pallas import tpu as pltpu
from jax.sharding import PartitionSpec as P

MESH = pl.DeviceIdType.MESH
VMEM_LIMIT = 56 * 1024 * 1024


def place(axis, count):
    me = lax.axis_index(axis)
    return me, me // 2, lax.rem(me, 2), count // 2


def greet(axis, count):
    me, z, y, length = place(axis, count)
    barrier = pltpu.get_barrier_semaphore()

    def signal(device):
        pl.semaphore_signal(barrier, inc=1, device_id={axis: device}, device_id_type=MESH)

    signal(me + 1 - 2 * y)
    pl.when(z > 0)(lambda: signal(me - 2))
    pl.when(z < length - 1)(lambda: signal(me + 2))
    pl.semaphore_wait(barrier, 1 + (z > 0).astype(jnp.int32) + (z < length - 1).astype(jnp.int32))


def gather(axis, count, causal, own, out, line_sem, side_sem, recv_sem, work=None):
    me, z, y, length = place(axis, count)
    other = 1 - y

    def copy(block, source, device, sem):
        return pltpu.make_async_remote_copy(
            src_ref=source, dst_ref=out.at[block], send_sem=sem, recv_sem=recv_sem.at[block],
            device_id={axis: device}, device_id_type=MESH)

    def across(line, source):
        return copy(line * 2 + y, source, z * 2 + other, side_sem.at[line])

    def right(line, source):
        return copy(line * 2 + y, source, me + 2, line_sem.at[0, line])

    def left(line, source):
        return copy(line * 2 + y, source, me - 2, line_sem.at[1, line])

    def arrived(block):
        copy(block, own, me, side_sem.at[0]).wait_recv()

    def own_across():
        return (y == 0) if causal else (y >= 0)

    pl.when(z < length - 1)(lambda: right(z, own).start())
    if not causal:
        pl.when(z > 0)(lambda: left(z, own).start())
    pl.when(own_across())(lambda: across(z, own).start())
    for step in range(1, length):
        @pl.when(z - step >= 0)
        def _():
            line = z - step
            block = line * 2 + y
            arrived(block)
            pl.when(z < length - 1)(lambda: right(line, out.at[block]).start())
            across(line, out.at[block]).start()

        if not causal:
            @pl.when(z + step < length)
            def _():
                line = z + step
                block = line * 2 + y
                arrived(block)
                pl.when(z > 0)(lambda: left(line, out.at[block]).start())
                across(line, out.at[block]).start()

        if work is not None:
            if step == 1:
                work(z)
            else:
                pl.when(z - step + 1 >= 0)(lambda: work(z - step + 1))
                pl.when(z + step - 1 < length)(lambda: work(z + step - 1))

    if work is not None:
        last = length - 1
        if last == 0:
            work(z)
        else:
            pl.when(z - last >= 0)(lambda: work(z - last))
            pl.when(z + last < length)(lambda: work(z + last))

    for line in range(length):
        if work is None:
            @pl.when((line < z) | ((line == z) & (y == 1)) if causal else (z >= 0))
            def _():
                arrived(line * 2 + other)

        @pl.when((line < z) | ((line == z) & (y == 0)) if causal else (z >= 0))
        def _():
            across(line, own).wait_send()

        pl.when((line <= z) & (z < length - 1))(lambda: right(line, own).wait_send())
        if not causal:
            pl.when((line >= z) & (z > 0))(lambda: left(line, own).wait_send())


def gather_sems(count):
    return [
        pltpu.SemaphoreType.DMA((2, count // 2)),
        pltpu.SemaphoreType.DMA((count // 2,)),
        pltpu.SemaphoreType.DMA((count,)),
    ]


def encode_kernel(
    feat_count, layer_count, own, enc_hbm, mask, full_out, features_out,
    full, enc, features, local_sem, layer_sem, line_sem, side_sem, recv_sem,
    right_send, across_send, feature_recv,
):
    me, z, y, length = place("feat", feat_count)
    layer, chip, core, chips = place("layer", layer_count)
    rows, width = own.shape
    tile = min(256, enc.shape[0])
    group = 2 if rows % 16 == 0 else 1
    enc_copy = pltpu.make_async_copy(enc_hbm, enc, local_sem.at[0])
    enc_copy.start()
    own_copy = pltpu.make_async_copy(own, full.at[me], local_sem.at[1])
    own_copy.start()

    barrier = pltpu.get_barrier_semaphore()

    def signal(axis, device):
        pl.semaphore_signal(barrier, inc=1, device_id={axis: device}, device_id_type=MESH)

    signal("feat", me + 1 - 2 * y)
    signal("layer", layer + 1 - 2 * core)
    pl.when(z > 0)(lambda: signal("feat", me - 2))
    pl.when(z < length - 1)(lambda: signal("feat", me + 2))
    pl.when(chip > 0)(lambda: signal("layer", layer - 2))
    pl.when(chip < chips - 1)(lambda: signal("layer", layer + 2))
    pl.semaphore_wait(
        barrier,
        2 + (z > 0).astype(jnp.int32) + (z < length - 1).astype(jnp.int32)
        + (chip > 0).astype(jnp.int32) + (chip < chips - 1).astype(jnp.int32))

    def send(hop, line, sem, device):
        block = features.at[layer - 2 * hop, line]
        return pltpu.make_async_remote_copy(
            src_ref=block, dst_ref=block, send_sem=sem.at[hop, line],
            recv_sem=feature_recv.at[layer - 2 * hop, line],
            device_id={"layer": device}, device_id_type=MESH)

    def right(hop, line):
        return send(hop, line, right_send, layer + 2)

    def across(hop, line):
        return send(hop, line, across_send, layer + 1 - 2 * core)

    def landed(source, line):
        block = features.at[source, line]
        pltpu.make_async_remote_copy(
            src_ref=block, dst_ref=block, send_sem=right_send.at[0, line],
            recv_sem=feature_recv.at[source, line],
            device_id={"layer": layer}, device_id_type=MESH).wait_recv()

    def relay(line):
        for hop in range(1, chips):
            @pl.when(chip >= hop)
            def _():
                landed(layer - 2 * hop, line)
                pl.when(chip < chips - 1)(lambda: right(hop, line).start())
                across(hop, line).start()

    def work(line):
        @pl.when(line == z)
        def _():
            enc_copy.wait()
            own_copy.wait()

        pltpu.make_async_remote_copy(
            src_ref=own, dst_ref=full.at[line * 2 + 1 - y], send_sem=side_sem.at[0],
            recv_sem=recv_sem.at[line * 2 + 1 - y],
            device_id={"feat": me}, device_id_type=MESH).wait_recv()

        @pl.loop(0, enc.shape[0] // tile)
        def _(index):
            at = pl.ds(pl.multiple_of(index * tile, tile), tile)
            for part in range(2 // group):
                block = full[pl.ds(line * 2 + part, group)].reshape(group * rows, width)
                acts = lax.dot_general(
                    block, enc[at, :], (((1,), (1,)), ((), ())),
                    preferred_element_type=jnp.float32)
                tokens = pl.ds(part * rows, group * rows)
                kept = mask[line, tokens, at].astype(jnp.float32) * acts
                features[layer, line, tokens, at] = kept.astype(features.dtype)

        pl.when(chip < chips - 1)(lambda: right(0, line).start())
        pl.when(core == 0)(lambda: across(0, line).start())

    for source in range(layer_count):
        @pl.when(source > layer)
        def _():
            features[source] = jnp.zeros(features.shape[1:], features.dtype)

    gather("feat", feat_count, False, own, full, line_sem, side_sem, recv_sem, work)
    full_copy = pltpu.make_async_copy(full, full_out, local_sem.at[0])
    full_copy.start()
    relay(z)
    for step in range(1, length):
        pl.when(z - step >= 0)(lambda: relay(z - step))
        pl.when(z + step < length)(lambda: relay(z + step))
    for line in range(length):
        pl.when(core == 1)(lambda: landed(layer - 1, line))
        for hop in range(1, chips):
            pl.when(chip >= hop)(lambda: landed(layer - 2 * hop + 1 - 2 * core, line))
        for hop in range(chips):
            @pl.when(chip >= hop)
            def _():
                pl.when(chip < chips - 1)(lambda: right(hop, line).wait_send())
                if hop == 0:
                    pl.when(core == 0)(lambda: across(hop, line).wait_send())
                else:
                    across(hop, line).wait_send()

    def out_copy(source):
        return pltpu.make_async_copy(
            features.at[source], features_out.at[source], layer_sem.at[source])

    for source in range(layer_count):
        out_copy(source).start()
    for source in range(layer_count):
        out_copy(source).wait()
    full_copy.wait()


def encode_call(sources, enc_weight, mask, collective_id):
    count, layers = lax.axis_size("feat"), lax.axis_size("layer")
    rows, width = sources.shape
    size = enc_weight.shape[0]
    length, chips = count // 2, layers // 2
    hbm = pl.BlockSpec(memory_space=pl.ANY)
    full_shape = (count, rows, width)
    feature_shape = (layers, length, 2 * rows, size)
    return pl.pallas_call(
        functools.partial(encode_kernel, count, layers),
        out_shape=(
            jax.ShapeDtypeStruct(full_shape, sources.dtype),
            jax.ShapeDtypeStruct(feature_shape, sources.dtype),
        ),
        in_specs=[hbm, hbm, pl.BlockSpec(memory_space=pltpu.VMEM)],
        out_specs=(hbm, hbm),
        scratch_shapes=[
            pltpu.VMEM(full_shape, sources.dtype),
            pltpu.VMEM(enc_weight.shape, sources.dtype),
            pltpu.VMEM(feature_shape, sources.dtype),
            pltpu.SemaphoreType.DMA((2,)),
            pltpu.SemaphoreType.DMA((layers,)),
        ] + gather_sems(count) + [
            pltpu.SemaphoreType.DMA((chips, length)),
            pltpu.SemaphoreType.DMA((chips, length)),
            pltpu.SemaphoreType.DMA((layers, length)),
        ],
        compiler_params=pltpu.CompilerParams(
            collective_id=collective_id, has_side_effects=True, vmem_limit_bytes=VMEM_LIMIT),
    )(sources, enc_weight, mask.reshape(length, 2 * rows, size))


def reduce_kernel(
    axis, count, scale, parts, targets, errors, full,
    from_side, from_left, from_right, to_right, to_left, scaled,
    local_sem, line_sem, side_sem, recv_sem,
    side_send, side_recv, right_send, right_recv, left_send, left_recv,
):
    me, z, y, length = place(axis, count)
    rows = targets.shape[0]
    step_rows = min(16, rows)
    greet(axis, count)

    def copy(source, target, send_sem, recv, device):
        return pltpu.make_async_remote_copy(
            src_ref=source, dst_ref=target, send_sem=send_sem, recv_sem=recv,
            device_id={axis: device}, device_id_type=MESH)

    def side(line):
        return copy(parts.at[line * 2 + 1 - y], from_side.at[line], side_send.at[line],
                    side_recv.at[line], me + 1 - 2 * y)

    def right(line):
        return copy(to_right.at[line], from_left.at[line], right_send.at[line],
                    right_recv.at[line], me + 2)

    def left(line):
        return copy(to_left.at[line], from_right.at[line], left_send.at[line],
                    left_recv.at[line], me - 2)

    for step in range(length - 1):
        pl.when(length - 1 - step > z)(lambda: side(length - 1 - step).start())
        pl.when(step < z)(lambda: side(step).start())
    side(z).start()

    def add(line, others, store):
        @pl.loop(0, rows // step_rows)
        def _(index):
            at = pl.ds(pl.multiple_of(index * step_rows, step_rows), step_rows)
            total = parts[line * 2 + y, at, :].astype(jnp.float32)
            for ref in others:
                total += ref[line, at, :].astype(jnp.float32)
            store(at, total)

    def pass_on(line, incoming, has_incoming, outgoing, message, recv):
        def store(at, total):
            outgoing[line, at, :] = total.astype(outgoing.dtype)

        side(line).wait_recv()

        @pl.when(has_incoming)
        def _():
            recv(line).wait_recv()
            add(line, (from_side, incoming), store)

        @pl.when(jnp.logical_not(has_incoming))
        def _():
            add(line, (from_side,), store)

        message(line).start()

    for step in range(length - 1):
        @pl.when(length - 1 - step > z)
        def _():
            pass_on(length - 1 - step, from_left, z > 0, to_right, right, right)

        @pl.when(step < z)
        def _():
            pass_on(step, from_right, z < length - 1, to_left, left, left)

    side(z).wait_recv()

    def finish(others):
        def store(at, total):
            error = total - targets[at, :].astype(jnp.float32)
            errors[at, :] = error
            scaled[at, :] = (error * scale).astype(scaled.dtype)

        add(z, others, store)

    @pl.when(z > 0)
    def _():
        right(z).wait_recv()

    @pl.when(z < length - 1)
    def _():
        left(z).wait_recv()

    pl.when((z > 0) & (z < length - 1))(lambda: finish((from_side, from_left, from_right)))
    pl.when((z > 0) & (z == length - 1))(lambda: finish((from_side, from_left)))
    pl.when((z == 0) & (z < length - 1))(lambda: finish((from_side, from_right)))
    pl.when((z == 0) & (z == length - 1))(lambda: finish((from_side,)))

    local = pltpu.make_async_copy(scaled, full.at[me], local_sem)
    local.start()
    gather(axis, count, False, scaled, full, line_sem, side_sem, recv_sem)
    local.wait()
    for line in range(length):
        side(line).wait_send()
        pl.when(line > z)(lambda: right(line).wait_send())
        pl.when(line < z)(lambda: left(line).wait_send())


def reduce_call(parts, targets, axis, scale, collective_id):
    count, rows, width = parts.shape
    length = count // 2
    lane = pltpu.VMEM((length, rows, width), parts.dtype)
    sems = pltpu.SemaphoreType.DMA((length,))
    vmem = pl.BlockSpec(memory_space=pltpu.VMEM)
    return pl.pallas_call(
        functools.partial(reduce_kernel, axis, count, scale),
        out_shape=(
            jax.ShapeDtypeStruct((rows, width), jnp.float32),
            jax.ShapeDtypeStruct((count, rows, width), parts.dtype),
        ),
        in_specs=[vmem, vmem],
        out_specs=(vmem, pl.BlockSpec(memory_space=pl.ANY)),
        scratch_shapes=[lane] * 5 + [pltpu.VMEM((rows, width), parts.dtype)]
        + [pltpu.SemaphoreType.DMA(())] + gather_sems(count) + [sems] * 6,
        compiler_params=pltpu.CompilerParams(
            collective_id=collective_id, has_side_effects=True, vmem_limit_bytes=VMEM_LIMIT),
    )(parts, targets)


def scatter_layers(partial):
    layers = lax.axis_size("layer")
    layer, chip, core, chips = place("layer", layers)
    pairs = partial.reshape((chips, 2) + partial.shape[1:])
    swap = [(device, device ^ 1) for device in range(layers)]
    given = lax.ppermute(lax.dynamic_index_in_dim(pairs, 1 - core, 1, keepdims=False), "layer", swap)
    kept = lax.dynamic_index_in_dim(pairs, core, 1, keepdims=False)
    sums = (kept.astype(jnp.float32) + given.astype(jnp.float32)).astype(partial.dtype)
    total = lax.dynamic_index_in_dim(sums, chip, 0, keepdims=False).astype(jnp.float32)
    for shift in range(1, chips):
        target = lax.rem(chip + shift, chips)
        moves = [(device, (device + 2 * shift) % layers) for device in range(layers)]
        sent = lax.dynamic_index_in_dim(sums, target, 0, keepdims=False)
        total += lax.ppermute(sent, "layer", moves).astype(jnp.float32)
    return total


def on_device(sources, targets, enc_weight, dec_weight, active):
    layer_count = dec_weight.shape[1]
    target_pos = lax.axis_index("layer")
    rows, width = sources.shape[1:]
    feat = lax.axis_size("feat")
    tokens = rows * feat
    mask = active[0].astype(jnp.bfloat16).T
    source_full, all_features = encode_call(sources[0], enc_weight[0], mask, 0)
    source_full = source_full.reshape(tokens, width)
    all_features = all_features.reshape(layer_count, tokens, -1)
    causal = (jnp.arange(layer_count, dtype=jnp.int32) <= target_pos)[:, None, None]
    recon = jnp.einsum(
        "ltf,lfd->td", all_features, dec_weight[0], preferred_element_type=jnp.float32
    ).astype(jnp.bfloat16)
    errors, scaled = reduce_call(
        recon.reshape(feat, rows, width), targets[0], "feat", 1.0 / math.sqrt(tokens), 2
    )
    scaled_full = scaled.reshape(tokens, width)
    partial_grad = jnp.einsum(
        "lfd,td->lft", dec_weight[0], scaled_full, preferred_element_type=jnp.float32
    )
    partial_grad = jnp.where(causal, partial_grad, 0.0).astype(jnp.bfloat16)
    feature_grad = scatter_layers(partial_grad)
    grad_dec = jnp.einsum(
        "ltf,td->lfd", all_features, scaled_full, preferred_element_type=jnp.float32
    ).astype(jnp.bfloat16)
    pre_grad = (active[0].astype(jnp.float32) * feature_grad).astype(jnp.bfloat16)
    grad_enc = jnp.einsum(
        "ft,td->fd", pre_grad, source_full, preferred_element_type=jnp.float32
    ).astype(jnp.bfloat16)
    return (errors[None], grad_dec[None], grad_enc[None])


def solution(mesh):
    in_specs = (
        P("layer", "feat", None),
        P("layer", "feat", None),
        P("layer", "feat", None),
        P("layer", None, "feat", None),
        P("layer", "feat", None),
    )
    out_specs = (P("layer", "feat", None), P("layer", None, "feat", None), P("layer", "feat", None))
    return jax.shard_map(
        on_device, mesh=mesh, in_specs=in_specs, out_specs=out_specs, check_vma=False
    )
```
